128 devices in a mesh: section: 2 (over core), ctx: 16 (over y, x), tp: 4 (over z).
Axes of the slice: x: 4, y: 4, z: 4, core: 2. Of those that a mesh axis runs over, the one named last changes fastest.
Arguments:
- inputs: bfloat16 [2, 4096, 768], P(None, 'ctx'), may hold values from -6 to 6
- cotangent: bfloat16 [2, 4096, 768], P(None, 'ctx'), may hold values from -6 to 6
- segments: int32 [2, 4096], P(None, 'ctx'), may hold values from 0 to 5, never falling along the last dimension, each value on 1 to 2048 neighbouring positions
- w_qkv: bfloat16 [2, 768, 2304], P('section', 'ctx', 'tp'), may hold values from -0.21875 to 0.21875
- b_qkv: bfloat16 [2, 2304], P('section', 'tp'), may hold values from -3 to 3
- w_out: bfloat16 [2, 768, 768], P('section', 'ctx', 'tp'), may hold values from -1.25 to 1.25
- w_up: bfloat16 [2, 768, 3072], P('section', 'ctx', 'tp'), may hold values from -0.21875 to 0.21875
- b_up: bfloat16 [2, 3072], P('section', 'tp'), may hold values from -3 to 3
- w_down: bfloat16 [2, 768, 3072], P('section', 'ctx', 'tp'), may hold values from -0.109375 to 0.109375
- b_out: bfloat16 [2, 768], P('section'), may hold values from -3 to 3
- norm_gain: bfloat16 [2, 2, 768], P('section'), may hold values from 0.5 to 1.5
- norm_bias: bfloat16 [2, 2, 768], P('section'), may hold values from -2 to 2
Outputs:
- hidden_out: bfloat16 [2, 2, 4096, 768], P('section', None, 'ctx')
- input_grad: float32 [2, 2, 4096, 768], P('section', None, 'ctx')
- grad_w_qkv: float32 [2, 768, 2304], P('section', 'ctx', 'tp')
- grad_b_qkv: float32 [2, 2304], P('section', 'tp')
- grad_w_out: float32 [2, 768, 768], P('section', 'ctx', 'tp')
- grad_w_up: float32 [2, 768, 3072], P('section', 'ctx', 'tp')
- grad_b_up: float32 [2, 3072], P('section', 'tp')
- grad_w_down: float32 [2, 768, 3072], P('section', 'ctx', 'tp')
- grad_b_out: float32 [2, 768], P('section')
- grad_norm_gain: float32 [2, 2, 768], P('section')
- grad_norm_bias: float32 [2, 2, 768], P('section')
The draws below stay inside these ranges and needn't reach their ends.
Inputs may be any that keep to these rules, and one draw needn't show every extreme that they name: `segments`: document ids of each micro-batch never fall along its tokens; every id occurs, each document has 1 to 2048 tokens and one has exactly 2048.
All inputs are finite; a program needn't handle non-finite values.
Results may differ from the reference program's by a relative error of at most 0.02.
Values may be sent and summed in bfloat16 or wider, within the bound.
No kernel may reach another device: no remote copies, remote signals or barrier semaphores. Data moves between devices by JAX's collectives and lax.ppermute only.
A program may use at most 128 MiB of HBM per device.

```python
import math
import jax
import jax.numpy as jnp
import numpy as np
from jax import lax

D = 768
HEADS = 12
HEAD_DIM = 64
ROT = 16
FF = 3072
MB = 2
DOCS = 6
LEN = 4096
MAXDOC = 2048


def block_levels(stream_key, extent, pieces, smallest, top_value):
    def one(position, shards_of):
        heights = jax.random.uniform(jax.random.fold_in(jax.random.fold_in(stream_key, 6), position), (shards_of,), jnp.float32, smallest / len(pieces), top_value / len(pieces))
        return jnp.repeat(jnp.exp(heights), extent[position] // shards_of).reshape((-1,) + (1,) * (len(extent) - position - 1))

    level = one(*pieces[0])
    for cut in pieces[1:]:
        level = level * one(*cut)
    return level


def split_up(count, total, bound, slope):
    weights = [(1 << 20) // math.isqrt(grade ** slope) + 1 for grade in range(2, count + 1)]
    surplus, given = total - bound - (count - 1), [1] * (count - 1)
    while surplus > 0:
        movable = [i for i in range(count - 1) if given[i] < bound]
        pool, remaining = sum([weights[i] for i in movable]), surplus
        for i in movable:
            extra = min(bound - given[i], max(1, remaining * weights[i] // pool), surplus)
            given[i] = given[i] + extra
            surplus = surplus - extra
    return np.array([bound] + given)


def uneven(stream_key, number_of, total, most, skew):
    if number_of == 2:
        one = jax.random.randint(stream_key, (), max(1, total - most), min(most, total - 1) + 1)
        return jnp.stack([one, total - one])
    sizes = jnp.asarray(split_up(number_of, total, most, skew), jnp.int32)
    pairs = (number_of - 1) // 2
    source_of, taker = sizes[1:1 + 2 * pairs:2], sizes[2:2 + 2 * pairs:2]
    margin = jnp.minimum(source_of - 1, most - taker)
    moved = jax.random.randint(jax.random.fold_in(stream_key, 1), (pairs,), 0, 1 << 20) % (margin + 1)
    sizes = sizes.at[1:1 + 2 * pairs:2].set(source_of - moved).at[2:2 + 2 * pairs:2].set(taker + moved)
    return sizes[jax.random.permutation(jax.random.fold_in(stream_key, 2), number_of)]


def bell_draw(rng, shape, width, bound, shards=(), held_as=jnp.bfloat16):
    drawn = jax.random.normal(rng, shape, jnp.float32) * width
    if len(shards) > 0:
        drawn = block_levels(rng, shape, shards, -0.22, 0.18) * drawn
    return jnp.clip(drawn, min=-bound, max=bound).astype(held_as)


def setup_inputs(seed: int = 0) -> dict:
    streams_of = jax.random.split(jax.random.key(seed), 13)
    return {
        "inputs": bell_draw(streams_of[0], (MB, LEN, D), 1.0, 6.0, ((1, 16),)),
        "cotangent": bell_draw(streams_of[1], (MB, LEN, D), 1.0, 6.0, ((1, 16),)),
        "segments": jax.vmap(lambda own: jnp.searchsorted(jnp.cumsum(uneven(own, DOCS, LEN, MAXDOC, 2)), jnp.arange(LEN), side="right"))(jax.random.split(streams_of[2], MB)).reshape((MB, LEN)).astype(jnp.int32),
        "w_qkv": bell_draw(streams_of[3], (2, D, 3 * D), D ** -0.5, 0.21875, ((0, 2), (1, 16), (2, 4))),
        "b_qkv": bell_draw(streams_of[4], (2, 3 * D), 0.5, 3.0, ((0, 2), (1, 4))),
        "w_out": bell_draw(streams_of[5], (2, D, D), (D // 32) ** -0.5, 1.25, ((0, 2), (1, 16), (2, 4))),
        "w_up": bell_draw(streams_of[6], (2, D, FF), D ** -0.5, 0.21875, ((0, 2), (1, 16), (2, 4))),
        "b_up": bell_draw(streams_of[7], (2, FF), 0.5, 3.0, ((0, 2), (1, 4))),
        "w_down": bell_draw(streams_of[8], (2, D, FF), FF ** -0.5, 0.109375, ((0, 2), (1, 16), (2, 4))),
        "b_out": bell_draw(streams_of[9], (2, D), 0.5, 3.0, ((0, 2),)),
        "norm_gain": jnp.clip(1.0 + 0.1 * jax.random.normal(streams_of[10], (2, 2, D), jnp.float32), 0.5, 1.5).astype(jnp.bfloat16),
        "norm_bias": bell_draw(streams_of[11], (2, 2, D), 0.3, 2.0, ((0, 2),)),
    }


@jax.custom_vjp
def low(v):
    return lax.optimization_barrier(v.astype(jnp.bfloat16)).astype(jnp.float32)

@jax.custom_vjp
def low_back(v):
    return v

def low_keep(v):
    return (low(v), None)

def low_pass(kept, grad):
    return (grad,)

def back_keep(v):
    return (v, None)

def back_low(kept, grad):
    return (low(grad),)
low.defvjp(low_keep, low_pass)
low_back.defvjp(back_keep, back_low)

def matmul(left, right):
    return jnp.dot(left, right, precision=lax.Precision.HIGHEST, preferred_element_type=jnp.float32)

def layer_norm(values, gain_vec, shift_vec):
    center = values - lax.optimization_barrier(jnp.mean(values, axis=-1, keepdims=True))
    spread = lax.optimization_barrier(jnp.mean(center * center, axis=-1, keepdims=True))
    return center * lax.rsqrt(spread + 1e-05) * gain_vec + shift_vec

def angle_table(places):
    frequency = jnp.exp(-(jnp.arange(ROT // 2, dtype=jnp.float32) * (2.0 / ROT)) * jnp.log(10000.0))
    return places[:, None] * frequency[None, :]

def rotate(values, angles):
    half_rot = angles.shape[-1]
    cosine = jnp.cos(angles)
    sine_vals = jnp.sin(angles)
    cosine = jnp.concatenate([cosine, cosine], -1)[:, None, :]
    sine_vals = jnp.concatenate([sine_vals, sine_vals], -1)[:, None, :]
    rot_part = values[..., :2 * half_rot]
    turned = jnp.concatenate([-rot_part[..., half_rot:], rot_part[..., :half_rot]], -1)
    return jnp.concatenate([rot_part * cosine + turned * sine_vals, values[..., 2 * half_rot:]], -1)

def gelu_exact(values):
    return 0.5 * values * (1.0 + jax.scipy.special.erf(values * 0.7071067811865476))

def attention(query_heads, key_heads, value_heads, seg_ids):
    length = query_heads.shape[0]
    block_rows = math.gcd(length, 512)
    block_count = length // block_rows
    places = jnp.arange(length, dtype=jnp.int32)
    query_blocks = query_heads.reshape(block_count, block_rows, HEADS, HEAD_DIM)
    starts = jnp.arange(block_count, dtype=jnp.int32) * block_rows

    def one_block(items):
        query_block, start_row = items
        query_places = start_row + jnp.arange(block_rows, dtype=jnp.int32)
        query_segs = lax.dynamic_slice_in_dim(seg_ids, start_row, block_rows)
        scores = jnp.einsum('qhd,khd->hqk', query_block, key_heads, precision=lax.Precision.HIGHEST) * HEAD_DIM ** (-0.5)
        scores = low_back(scores)
        allowed = (places[None, :] <= query_places[:, None]) & (seg_ids[None, :] == query_segs[:, None])
        scores = jnp.where(allowed[None], scores, -1000000000.0)
        probs = jax.nn.softmax(scores, axis=-1)
        return jnp.einsum('hqk,khd->qhd', low(probs), value_heads, precision=lax.Precision.HIGHEST)
    mixed_heads = lax.map(jax.checkpoint(one_block), (query_blocks, starts))
    return mixed_heads.reshape(length, HEADS * HEAD_DIM)

def block_layer(layer_in, seg_ids, params):
    w_qkv, b_qkv, w_out, w_up, b_up, w_down, b_out, norm_gain, norm_bias = params
    length = layer_in.shape[0]
    first_in = low(layer_norm(layer_in, norm_gain[0], norm_bias[0]))
    second_in = low(layer_norm(layer_in, norm_gain[1], norm_bias[1]))
    packed = low_back(matmul(first_in, w_qkv) + b_qkv).reshape(length, HEADS, 3, HEAD_DIM)
    angles = angle_table(jnp.arange(length, dtype=jnp.float32))
    query_heads = low(rotate(packed[:, :, 0], angles))
    key_heads = low(rotate(packed[:, :, 1], angles))
    value_heads = low(packed[:, :, 2])
    mixed_heads = attention(query_heads, key_heads, value_heads, seg_ids)
    mixed_heads = low_back(low(mixed_heads))
    attended = matmul(mixed_heads, w_out.T)
    hidden_pre = low_back(matmul(second_in, w_up) + b_up)
    hidden = low(gelu_exact(hidden_pre))
    return layer_in + attended + matmul(hidden, w_down.T) + b_out

def reference(inputs, cotangent, segments, w_qkv, b_qkv, w_out, w_up, b_up, w_down, b_out, norm_gain, norm_bias):
    params = tuple((item.astype(jnp.float32) for item in (w_qkv, b_qkv, w_out, w_up, b_up, w_down, b_out, norm_gain, norm_bias)))
    start_values = inputs.astype(jnp.float32)
    offsets = jnp.zeros(inputs.shape, jnp.float32)

    def forward(start_values, params, offsets):
        first_outs = []
        last_outs = []
        lower_params = tuple((item[0] for item in params))
        upper_params = tuple((item[1] for item in params))
        for micro_index in range(MB):
            middle_value = low_back(low(block_layer(start_values[micro_index], segments[micro_index], lower_params))) + offsets[micro_index]
            first_outs.append(middle_value)
            last_outs.append(low(block_layer(middle_value, segments[micro_index], upper_params)))
        return (jnp.stack(first_outs), jnp.stack(last_outs))
    (middle_all, final_all), pullback = jax.vjp(forward, start_values, params, offsets)
    grad_start, grad_params, grad_middle = pullback((jnp.zeros_like(middle_all), cotangent.astype(jnp.float32)))
    hidden_out = jnp.stack([middle_all, final_all]).astype(jnp.bfloat16)
    input_grad = jnp.stack([grad_start, grad_middle])
    return (hidden_out, input_grad, grad_params[0], grad_params[1], grad_params[2], grad_params[3], grad_params[4], grad_params[5], grad_params[6], grad_params[7], grad_params[8])
```

```python
import functools

import jax
import jax.numpy as jnp
from jax import lax
from jax.experimental import pallas as pl
from jax.experimental.pallas import tpu as pltpu
from jax.sharding import PartitionSpec as P

HEAD_DIM = 64
ROT = 16
BLOCKS = 9
CHIPS = 16
F32 = jnp.float32
BF16 = jnp.bfloat16
FAR = -1e30


def batch_of(chip):
    return (chip ^ (chip >> 1)) & 1


def dot(left, right):
    return jnp.dot(left, right, preferred_element_type=F32)


def dot_last(left, right):
    return lax.dot_general(left, right, (((1,), (1,)), ((), ())), preferred_element_type=F32)


def dot_first(left, right):
    return lax.dot_general(left, right, (((0,), (0,)), ((), ())), preferred_element_type=F32)


def moved(value, target):
    pairs = []
    for core in range(2):
        for chip in range(CHIPS):
            place = target(core, chip)
            if place is not None:
                pairs.append((core * CHIPS + chip, place[0] * CHIPS + place[1]))
    return lax.ppermute(value, ("section", "ctx"), pairs)


def swapped(value):
    return lax.ppermute(value, "section", [(0, 1), (1, 0)])


def chip_at(index, batch):
    low = 2 * index
    return low if batch_of(low) == batch else low + 1


def shifted(value, steps):
    def target(core, chip):
        index = chip // 2 + steps
        return (core, chip_at(index, batch_of(chip))) if 0 <= index < CHIPS // 2 else None

    return moved(value, target)


def to_home(value):
    return moved(value, lambda core, chip: (batch_of(chip), (chip & ~1) + core))


def from_home(value):
    return moved(value, lambda core, chip: (core, chip ^ 1) if chip % 2 == core else None)


def source(g_ref, r_ref, block):
    ref = g_ref if block % 2 == 0 else r_ref
    return ref, slice((block // 2) * 256, (block // 2) * 256 + 256)


def attend_kernel(q_ref, g_ref, r_ref, qs_ref, ks_ref, o_ref, l_ref, bias_ref, s_ref):
    tile = (256, 256)
    for block in range(BLOCKS):
        cols = slice(block * 256, block * 256 + 256)
        allowed = qs_ref[...] == ks_ref[:, cols]
        if block == BLOCKS - 1:
            rows_of = lax.broadcasted_iota(jnp.int32, tile, 0)
            allowed = allowed & (lax.broadcasted_iota(jnp.int32, tile, 1) <= rows_of)
        bias_ref[:, cols] = jnp.where(allowed, 0.0, FAR)
    heads = q_ref.shape[1] // HEAD_DIM
    for head in range(heads):
        span = slice(head * HEAD_DIM, head * HEAD_DIM + HEAD_DIM)
        vspan = slice((heads + head) * HEAD_DIM, (heads + head) * HEAD_DIM + HEAD_DIM)
        query = q_ref[:, span]
        top = None
        for block in range(BLOCKS):
            cols = slice(block * 256, block * 256 + 256)
            ref, rows = source(g_ref, r_ref, block)
            scores = dot_last(query, ref[rows, span]) + bias_ref[:, cols]
            s_ref[:, cols] = scores
            top = scores if top is None else jnp.maximum(top, scores)
        top = jnp.max(top, axis=1, keepdims=True)
        total = jnp.zeros(tile, F32)
        mixed = jnp.zeros((256, HEAD_DIM), F32)
        for block in range(BLOCKS):
            cols = slice(block * 256, block * 256 + 256)
            ref, rows = source(g_ref, r_ref, block)
            weights = jnp.exp(s_ref[:, cols] - top)
            total = total + weights
            mixed = mixed + dot(weights.astype(BF16), ref[rows, vspan])
        total = jnp.sum(total, axis=1, keepdims=True)
        o_ref[:, span] = mixed / total
        l_ref[:, head : head + 1] = top + jnp.log(total)


def attend_back_kernel(
    q_ref, g_ref, r_ref, do_ref, lse_ref, delta_ref, qs_ref, ks_ref, dq_ref, dg_ref, dr_ref, bias_ref
):
    tile = (256, 256)
    for block in range(BLOCKS):
        rows = slice(block * 256, block * 256 + 256)
        allowed = ks_ref[rows, :] == qs_ref[...]
        if block == BLOCKS - 1:
            keys_of = lax.broadcasted_iota(jnp.int32, tile, 0)
            allowed = allowed & (keys_of <= lax.broadcasted_iota(jnp.int32, tile, 1))
        bias_ref[rows, :] = jnp.where(allowed, 0.0, FAR)
    heads = q_ref.shape[1] // HEAD_DIM
    for head in range(heads):
        span = slice(head * HEAD_DIM, head * HEAD_DIM + HEAD_DIM)
        vspan = slice((heads + head) * HEAD_DIM, (heads + head) * HEAD_DIM + HEAD_DIM)
        query = q_ref[:, span]
        grad_out = do_ref[:, span]
        lse = lse_ref[head : head + 1, :]
        delta = delta_ref[head : head + 1, :]
        grad_query = jnp.zeros((HEAD_DIM, 256), F32)
        for block in range(BLOCKS):
            ref, rows = source(g_ref, r_ref, block)
            out = dg_ref if block % 2 == 0 else dr_ref
            keys = ref[rows, span]
            scores = dot_last(keys, query) + bias_ref[block * 256 : block * 256 + 256, :]
            probs = jnp.exp(scores - lse)
            grad_probs = dot_last(ref[rows, vspan], grad_out)
            grad_scores = (probs * (grad_probs - delta)).astype(BF16)
            out[rows, span] = dot(grad_scores, query).astype(BF16)
            out[rows, vspan] = dot(probs.astype(BF16), grad_out).astype(BF16)
            grad_query = grad_query + dot_first(keys, grad_scores)
        dq_ref[span, :] = grad_query * (HEAD_DIM**-0.5)


def in_vmem(count):
    return [pl.BlockSpec(memory_space=pltpu.VMEM)] * count


def attend(query, g, r, qs, ks):
    return pl.pallas_call(
        attend_kernel,
        out_shape=(
            jax.ShapeDtypeStruct((256, query.shape[1]), F32),
            jax.ShapeDtypeStruct((256, 128), F32),
        ),
        in_specs=in_vmem(5),
        out_specs=tuple(in_vmem(2)),
        scratch_shapes=[pltpu.VMEM((256, BLOCKS * 256), F32), pltpu.VMEM((256, BLOCKS * 256), F32)],
        compiler_params=pltpu.CompilerParams(vmem_limit_bytes=40 * 1024 * 1024),
        cost_estimate=pl.CostEstimate(
            flops=2_000_000_000, bytes_accessed=3_000_000, transcendentals=1_800_000
        ),
    )(query, g, r, qs, ks)


def attend_back(query, g, r, grad_out, lse, delta, qs, ks):
    return pl.pallas_call(
        attend_back_kernel,
        out_shape=(
            jax.ShapeDtypeStruct((query.shape[1], 256), F32),
            jax.ShapeDtypeStruct(g.shape, BF16),
            jax.ShapeDtypeStruct(r.shape, BF16),
        ),
        in_specs=in_vmem(8),
        out_specs=tuple(in_vmem(3)),
        scratch_shapes=[pltpu.VMEM((BLOCKS * 256, 256), F32)],
        compiler_params=pltpu.CompilerParams(vmem_limit_bytes=40 * 1024 * 1024),
        cost_estimate=pl.CostEstimate(
            flops=6_000_000_000, bytes_accessed=6_000_000, transcendentals=1_800_000
        ),
    )(query, g, r, grad_out, lse, delta, qs, ks)


def rotary_tables(first, count, heads):
    frequency = jnp.exp(-(jnp.arange(ROT // 2, dtype=F32) * (2.0 / ROT)) * jnp.log(10000.0))
    places = (first + jnp.arange(count, dtype=jnp.int32)).astype(F32)
    angles = places[:, None] * frequency[None, :]
    cosine, sine = jnp.cos(angles), jnp.sin(angles)
    ones = jnp.ones((count, HEAD_DIM - ROT), F32)
    zeros = jnp.zeros((count, HEAD_DIM - ROT), F32)
    cos_row = jnp.concatenate([cosine, cosine, ones], 1)
    sin_row = jnp.concatenate([-sine, sine, zeros], 1)
    return jnp.tile(cos_row, (1, heads)), jnp.tile(sin_row, (1, heads))


def turned(values):
    half = ROT // 2
    up = jnp.concatenate([values[:, half:], values[:, :half]], 1)
    down = jnp.concatenate([values[:, -half:], values[:, :-half]], 1)
    low = (lax.broadcasted_iota(jnp.int32, values.shape, 1) % HEAD_DIM) < half
    return jnp.where(low, up, down)


def rotate(values, tables, sign):
    return values * tables[0] + turned(values) * (sign * tables[1])


def gelu(values):
    return 0.5 * values * (1.0 + lax.erf(values * 0.7071067811865476))


def gelu_slope(values):
    return (
        0.5 * (1.0 + lax.erf(values * 0.7071067811865476))
        + values * jnp.exp(-0.5 * values * values) * 0.3989422804014327
    )


def tp_scatter(values):
    parts = values.astype(BF16).reshape(4, 64, values.shape[1])
    parts = lax.all_to_all(parts, "tp", 0, 0, tiled=True)
    return jnp.sum(parts.astype(F32), axis=0)


def tp_gather(rows):
    spread = jnp.broadcast_to(rows[None], (4,) + rows.shape)
    return lax.all_to_all(spread, "tp", 0, 0, tiled=True)


def per_device(
    inputs,
    cotangent,
    segments,
    w_qkv,
    b_qkv,
    w_out,
    w_up,
    b_up,
    w_down,
    b_out,
    norm_gain,
    norm_bias,
):
    core = lax.axis_index("section")
    chip = lax.axis_index("ctx")
    rank = lax.axis_index("tp")
    batch = batch_of(chip)
    shard = (chip & ~1) + core
    at_home = (chip % 2) == core
    tokens, width = inputs.shape[1], inputs.shape[2]
    qkv_cols, up_cols, att_cols = w_qkv.shape[2], w_up.shape[2], w_out.shape[2]
    heads = att_cols // HEAD_DIM
    part_rows = w_qkv.shape[1]

    def by_core(first, second):
        return jnp.where(core == 0, first, second)

    def of_layers(mine):
        other = swapped(mine)
        return by_core(mine, other), by_core(other, mine)

    def to_parts(cols):
        lead = cols.shape[:-1]
        return jnp.swapaxes(cols.reshape(lead + (heads, 3, HEAD_DIM)), -3, -2).reshape(cols.shape)

    def to_heads(cols):
        lead = cols.shape[:-1]
        return jnp.swapaxes(cols.reshape(lead + (3, heads, HEAD_DIM)), -3, -2).reshape(cols.shape)

    rows_at = rank * (tokens // 4)

    def own_rows(values):
        return lax.dynamic_slice_in_dim(values, rows_at, tokens // 4, 0)

    away_x = from_home(jnp.where(batch == 0, inputs[1], inputs[0]))
    first_x = jnp.where(at_home, jnp.where(batch == 0, inputs[0], inputs[1]), away_x)
    away_g = from_home(jnp.where(batch == 0, cotangent[1], cotangent[0]))
    last_g = jnp.where(at_home, jnp.where(batch == 0, cotangent[0], cotangent[1]), away_g)

    seg_row = jnp.concatenate(
        [segments.reshape(1, 2 * tokens).astype(BF16), jnp.zeros((1, qkv_cols - 2 * tokens), BF16)], 1
    )
    piece = jnp.concatenate(
        [to_parts(w_qkv[0]), seg_row, jnp.zeros((7, qkv_cols), BF16)], 0
    )
    spread = jnp.broadcast_to(piece[None], (CHIPS,) + piece.shape)
    spread = lax.all_to_all(spread, "ctx", 0, 0, tiled=True)
    weight_in = of_layers(spread[:, :part_rows].reshape(width, qkv_cols))
    all_segs = spread[:, part_rows, : 2 * tokens].astype(F32).reshape(CHIPS, 2, tokens)
    all_segs = jnp.where(batch == 0, all_segs[:, 0], all_segs[:, 1]).reshape(CHIPS * tokens)
    all_segs = jnp.concatenate([jnp.full(((BLOCKS - 1) * tokens,), -1.0, F32), all_segs])
    key_segs = lax.dynamic_slice_in_dim(all_segs, shard * tokens, BLOCKS * tokens)
    own_segs = key_segs[(BLOCKS - 1) * tokens :]

    rest = jnp.concatenate([w_up[0], w_out[0], w_down[0]], 1)
    rest = lax.all_gather(rest, "ctx", axis=0, tiled=True)
    small = jnp.concatenate(
        [
            jnp.concatenate([to_parts(b_qkv[0]), jnp.zeros((width - qkv_cols,), BF16)])[None],
            b_up,
            b_out,
            norm_gain[0],
            norm_bias[0],
            jnp.zeros((1, width), BF16),
        ],
        0,
    )
    smalls = of_layers(small)
    tables = rotary_tables(shard * tokens, tokens, heads)
    scale = HEAD_DIM**-0.5

    def forward(layer, x, rest):
        vectors = smalls[layer].astype(F32)
        bias_in, bias_up, bias_out = vectors[0, :qkv_cols], vectors[1], vectors[2]
        values = x.astype(F32)
        center = values - jnp.mean(values, axis=-1, keepdims=True)
        inverse = lax.rsqrt(jnp.mean(center * center, axis=-1, keepdims=True) + 1e-05)
        normed = center * inverse
        first_in = (normed * vectors[3] + vectors[5]).astype(BF16)
        second_in = (normed * vectors[4] + vectors[6]).astype(BF16)
        packed = dot(first_in, weight_in[layer]) + bias_in
        query = (rotate(packed[:, :att_cols], tables, 1.0).astype(BF16) * scale).astype(BF16)
        key = rotate(packed[:, att_cols : 2 * att_cols], tables, 1.0).astype(BF16)
        keyval = jnp.concatenate([key, packed[:, 2 * att_cols :].astype(BF16)], 1)
        g = jnp.concatenate([shifted(keyval, steps) for steps in (4, 3, 2, 1)] + [keyval], 0)
        r = swapped(by_core(g[tokens:], g[:-tokens]))
        if layer == 0:
            g, rest = lax.optimization_barrier((g, rest))
            rest = of_layers(rest)
        weight_up = rest[layer][:, :up_cols]
        weight_out = rest[layer][:, up_cols : up_cols + att_cols]
        weight_down = rest[layer][:, up_cols + att_cols :]
        mixed, lse = attend(query, g, r, own_segs[:, None], key_segs[None, :])
        hidden_pre = dot(second_in, weight_up) + bias_up
        hidden = gelu(hidden_pre).astype(BF16)
        mixed_low = mixed.astype(BF16)
        branches = dot_last(mixed_low, weight_out) + dot_last(hidden, weight_down)
        total = tp_scatter(branches)
        result = (own_rows(x).astype(F32) + total + bias_out).astype(BF16)
        result = tp_gather(result).reshape(tokens, width)
        kept = (normed, inverse, first_in, second_in, query, g, r, mixed, lse, hidden_pre, hidden)
        return result, kept, rest

    def backward(layer, grad_low, kept):
        normed, inverse, first_in, second_in, query, g, r, mixed, lse, hidden_pre, hidden = kept
        vectors = smalls[layer].astype(F32)
        weight_up = rest[layer][:, :up_cols]
        weight_out = rest[layer][:, up_cols : up_cols + att_cols]
        weight_down = rest[layer][:, up_cols + att_cols :]
        grad_mixed = dot(grad_low, weight_out).astype(BF16)
        delta = jnp.sum(
            (grad_mixed.astype(F32) * mixed).reshape(tokens, heads, HEAD_DIM), axis=-1
        )
        grad_pre = (dot(grad_low, weight_down) * gelu_slope(hidden_pre)).astype(BF16)
        grad_query, dg, dr = attend_back(
            query,
            g,
            r,
            grad_mixed,
            lse[:, :heads].T,
            delta.T,
            own_segs[None, :],
            key_segs[:, None],
        )
        partner = swapped(dr).astype(F32)
        zero = jnp.zeros((tokens, 2 * att_cols), F32)
        partner = by_core(
            jnp.concatenate([zero, partner], 0), jnp.concatenate([partner, zero], 0)
        )
        dg = dg.astype(F32) + partner
        sent = dg.astype(BF16)
        grad_keyval = dg[4 * tokens :]
        for slot in range(4):
            part = sent[slot * tokens : (slot + 1) * tokens]
            grad_keyval = grad_keyval + shifted(part, slot - 4).astype(F32)
        grad_packed = jnp.concatenate(
            [
                rotate(grad_query.T, tables, -1.0),
                rotate(grad_keyval[:, :att_cols], tables, -1.0),
                grad_keyval[:, att_cols:],
            ],
            1,
        ).astype(BF16)
        first_grad = dot_last(grad_packed, weight_in[layer])
        second_grad = dot_last(grad_pre, weight_up)
        scaled = tp_scatter(first_grad * vectors[3] + second_grad * vectors[4])
        rows_normed = own_rows(normed)
        grad_input = own_rows(grad_low).astype(F32) + own_rows(inverse) * (
            scaled
            - jnp.mean(scaled, axis=-1, keepdims=True)
            - rows_normed * jnp.mean(scaled * rows_normed, axis=-1, keepdims=True)
        )
        bias_in_grad = jnp.sum(grad_packed.astype(F32), axis=0)
        sums = jnp.stack(
            [
                jnp.concatenate([bias_in_grad, jnp.zeros((width - qkv_cols,), F32)]),
                jnp.sum(grad_pre.astype(F32), axis=0),
                jnp.sum(grad_low.astype(F32), axis=0),
                jnp.sum(first_grad * normed, axis=0),
                jnp.sum(second_grad * normed, axis=0),
                jnp.sum(first_grad, axis=0),
                jnp.sum(second_grad, axis=0),
                jnp.zeros((width,), F32),
            ]
        )
        weight_grad = jnp.concatenate(
            [
                dot_first(first_in, grad_packed).astype(BF16),
                dot_first(second_in, grad_pre).astype(BF16),
                dot_first(grad_low, mixed.astype(BF16)).astype(BF16),
                dot_first(grad_low, hidden).astype(BF16),
            ],
            1,
        )
        return grad_input, sums, weight_grad

    def core_halves(weight_grad):
        halves = weight_grad.reshape(CHIPS, 2, part_rows // 2, weight_grad.shape[1])
        got = swapped(by_core(halves[:, 1], halves[:, 0]))
        return (by_core(halves[:, 0], halves[:, 1]).astype(F32) + got.astype(F32)).astype(BF16)

    first_y, first_kept, rest = forward(0, first_x, rest)
    last_y, last_kept, rest = forward(1, first_y, rest)
    hidden_home = to_home(jnp.stack([first_y, last_y]))

    def weight_sums(weight_grad, sums):
        halves = core_halves(weight_grad)
        cols = weight_grad.shape[1]
        sums = sums + swapped(sums)
        high = sums.astype(BF16)
        fine = (sums - high.astype(F32)).astype(BF16)
        extra = jnp.concatenate([high, fine], 0).reshape(-1)
        extra = jnp.concatenate([extra, jnp.zeros((8 * cols - extra.shape[0],), BF16)])
        extra = jnp.broadcast_to(extra.reshape(1, 8, cols), (CHIPS, 8, cols))
        parcel = lax.all_to_all(jnp.concatenate([halves, extra], 1), "ctx", 0, 0, tiled=True)
        parcel = jnp.sum(parcel.astype(F32), axis=0)
        half = part_rows // 2
        both = parcel[half:].reshape(-1)[: 16 * width].reshape(2, 8, width)
        return parcel[:half], both[0] + both[1]

    top_grad, top_sums, top_weight = backward(1, last_g, last_kept)
    top_home = tp_gather(top_grad).reshape(tokens, width)
    middle = top_home.astype(BF16)
    top_home = to_home(top_home)
    top_weight, top_sums = weight_sums(top_weight, top_sums)

    low_grad, low_sums, low_weight = backward(0, middle, first_kept)
    low_home = to_home(low_grad)
    low_weight, low_sums = weight_sums(low_weight, low_sums)

    sums = by_core(low_sums, top_sums)
    final = jnp.concatenate([low_home, sums[3:7], jnp.zeros((4, width), F32)], 0)
    final = tp_gather(final)
    norms = jnp.sum(final[:, tokens // 4 : tokens // 4 + 4], axis=0)
    low_home = final[:, : tokens // 4].reshape(tokens, width)

    def two_batches(layers):
        mine = by_core(layers[0], layers[1])
        got = swapped(by_core(layers[1], layers[0]))
        return jnp.stack([by_core(mine, got), by_core(got, mine)])

    hidden_out = two_batches(hidden_home)[None]
    input_grad = two_batches((low_home, top_home))[None]
    mine = by_core(low_weight, top_weight)
    got = swapped(by_core(top_weight, low_weight))
    weight = jnp.concatenate([by_core(mine, got), by_core(got, mine)], 0)
    up_end = qkv_cols + up_cols
    out_end = up_end + att_cols
    return (
        hidden_out,
        input_grad,
        to_heads(weight[:, :qkv_cols])[None],
        to_heads(sums[0, :qkv_cols])[None],
        weight[:, up_end:out_end][None],
        weight[:, qkv_cols:up_end][None],
        sums[1][None],
        weight[:, out_end:][None],
        sums[2][None],
        norms[:2][None],
        norms[2:][None],
    )


def solution(mesh):
    placed = (
        P(None, "ctx", None),
        P(None, "ctx", None),
        P(None, "ctx"),
        P("section", "ctx", "tp"),
        P("section", "tp"),
        P("section", "ctx", "tp"),
        P("section", "ctx", "tp"),
        P("section", "tp"),
        P("section", "ctx", "tp"),
        P("section", None),
        P("section", None, None),
        P("section", None, None),
    )
    return jax.shard_map(
        per_device,
        mesh=mesh,
        in_specs=placed,
        out_specs=(
            P("section", None, "ctx", None),
            P("section", None, "ctx", None),
            P("section", "ctx", "tp"),
            P("section", "tp"),
            P("section", "ctx", "tp"),
            P("section", "ctx", "tp"),
            P("section", "tp"),
            P("section", "ctx", "tp"),
            P("section", None),
            P("section", None, None),
            P("section", None, None),
        ),
        check_vma=False,
    )
```

```python
import functools

import jax
import jax.numpy as jnp
from jax import lax
from jax.experimental import pallas as pl
from jax.experimental.pallas import tpu as pltpu
from jax.sharding import PartitionSpec as P

HEAD_DIM = 64
ROT = 16
BLOCKS = 9
CHIPS = 16
HEADS = 3
ATT = HEADS * HEAD_DIM
QKV = 3 * ATT
ROWS = 256
PART = 64
WIDTH = 768
UP = 768
REST = 2 * UP + 256
F32 = jnp.float32
BF16 = jnp.bfloat16
FAR = -1e30
SCALE = HEAD_DIM**-0.5
VMEM = pl.BlockSpec(memory_space=pltpu.VMEM)
ANY = pl.BlockSpec(memory_space=pl.ANY)


def batch_of(chip):
    return (chip ^ (chip >> 1)) & 1


def dot(left, right):
    return jnp.dot(left, right, preferred_element_type=F32)


def dot_last(left, right):
    return lax.dot_general(left, right, (((1,), (1,)), ((), ())), preferred_element_type=F32)


def dot_first(left, right):
    return lax.dot_general(left, right, (((0,), (0,)), ((), ())), preferred_element_type=F32)


def moved(value, target):
    pairs = []
    for core in range(2):
        for chip in range(CHIPS):
            place = target(core, chip)
            if place is not None:
                pairs.append((core * CHIPS + chip, place[0] * CHIPS + place[1]))
    return lax.ppermute(value, ("section", "ctx"), pairs)


def swapped(value):
    return lax.ppermute(value, "section", [(0, 1), (1, 0)])


def chip_at(index, batch):
    low = 2 * index
    return low if batch_of(low) == batch else low + 1


def shifted(value, steps):
    def target(core, chip):
        index = chip // 2 + steps
        return (core, chip_at(index, batch_of(chip))) if 0 <= index < CHIPS // 2 else None

    return moved(value, target)


def to_home(value):
    return moved(value, lambda core, chip: (batch_of(chip), (chip & ~1) + core))


def from_home(value):
    return moved(value, lambda core, chip: (core, chip ^ 1) if chip % 2 == core else None)


def call(body, outs, ins, specs, scratch, flops, exps=0):
    size = sum(item.size * item.dtype.itemsize for item in ins)
    size += sum(item.size * item.dtype.itemsize for item in outs)
    return pl.pallas_call(
        body,
        out_shape=tuple(outs),
        in_specs=specs,
        out_specs=tuple([VMEM] * len(outs)),
        scratch_shapes=scratch,
        compiler_params=pltpu.CompilerParams(vmem_limit_bytes=48 * 1024 * 1024),
        cost_estimate=pl.CostEstimate(flops=flops, bytes_accessed=size, transcendentals=exps),
    )(*ins)


def shape(rows, cols, dtype):
    return jax.ShapeDtypeStruct((rows, cols), dtype)


def pick_start(layer, mine, other, buffer, sem, cols=None):
    held = lax.axis_index("section") == layer

    def view(ref):
        return ref if cols is None else ref.at[:, pl.ds(cols[0], cols[1])]

    @pl.when(held)
    def _():
        pltpu.make_async_copy(view(mine), buffer, sem).start()

    @pl.when(jnp.logical_not(held))
    def _():
        pltpu.make_async_copy(view(other), buffer, sem).start()

    return pltpu.make_async_copy(view(mine), buffer, sem)


def turned(values):
    half = ROT // 2
    up = pltpu.roll(values, values.shape[1] - half, 1)
    down = pltpu.roll(values, half, 1)
    low = (lax.broadcasted_iota(jnp.int32, values.shape, 1) % HEAD_DIM) < half
    return jnp.where(low, up, down)


def gelu(values):
    return 0.5 * values * (1.0 + lax.erf(values * 0.7071067811865476))


def gelu_slope(values):
    return (
        0.5 * (1.0 + lax.erf(values * 0.7071067811865476))
        + values * jnp.exp(-0.5 * values * values) * 0.3989422804014327
    )


def project_kernel(
    layer, x_ref, v_ref, cos_ref, sin_ref, wa, wb, q_ref, kv_ref, a1_ref, a2_ref, n_ref, i_ref, w, sem
):
    copy = pick_start(layer, wa, wb, w, sem)
    values = x_ref[...].astype(F32)
    center = values - jnp.mean(values, axis=-1, keepdims=True)
    inverse = lax.rsqrt(jnp.mean(center * center, axis=-1, keepdims=True) + 1e-05)
    normed = center * inverse
    first_in = (normed * v_ref[3:4, :] + v_ref[5:6, :]).astype(BF16)
    a1_ref[...] = first_in
    a2_ref[...] = (normed * v_ref[4:5, :] + v_ref[6:7, :]).astype(BF16)
    n_ref[...] = normed
    i_ref[...] = jnp.broadcast_to(inverse, i_ref.shape)
    copy.wait()
    packed = dot(first_in, w[...]) + v_ref[0:1, :QKV]
    both = packed[:, : 2 * ATT]
    both = (both * cos_ref[...] + turned(both) * sin_ref[...]).astype(BF16)
    q_ref[...] = both[:, :ATT] * jnp.asarray(SCALE, BF16)
    kv_ref[:, :ATT] = both[:, ATT:]
    kv_ref[:, ATT:] = packed[:, 2 * ATT :].astype(BF16)


def project(layer, x, vectors, tables, weights):
    return call(
        functools.partial(project_kernel, layer),
        [
            shape(ROWS, ATT, BF16),
            shape(ROWS, 2 * ATT, BF16),
            shape(ROWS, WIDTH, BF16),
            shape(ROWS, WIDTH, BF16),
            shape(ROWS, WIDTH, F32),
            shape(ROWS, 128, F32),
        ],
        [x, vectors, *tables, *weights],
        [VMEM] * 4 + [ANY] * 2,
        [pltpu.VMEM((WIDTH, QKV), BF16), pltpu.SemaphoreType.DMA],
        300_000_000,
    )


def block_of(refs, block):
    if block % 2 == 0:
        return refs[block // 2], slice(0, ROWS)
    return refs[5], slice((block // 2) * ROWS, (block // 2) * ROWS + ROWS)


def spans(head):
    return (
        slice(head * HEAD_DIM, head * HEAD_DIM + HEAD_DIM),
        slice(ATT + head * HEAD_DIM, ATT + head * HEAD_DIM + HEAD_DIM),
    )


def attend_kernel(
    layer, q_ref, b0, b1, b2, b3, b4, br, qs_ref, ks_ref, a2_ref, v_ref, wa, wb,
    o_ref, l_ref, u_ref, h_ref, ob_ref, part_ref, bias_ref, s_ref, c_ref, w, sem,
):
    refs = (b0, b1, b2, b3, b4, br)
    copy = pick_start(layer, wa, wb, w, sem)
    tile = (ROWS, ROWS)
    for block in range(BLOCKS):
        cols = slice(block * ROWS, block * ROWS + ROWS)
        allowed = qs_ref[...] == ks_ref[:, cols]
        if block == BLOCKS - 1:
            rows_of = lax.broadcasted_iota(jnp.int32, tile, 0)
            allowed = allowed & (lax.broadcasted_iota(jnp.int32, tile, 1) <= rows_of)
        bias_ref[:, cols] = jnp.where(allowed, 0.0, FAR)
    c_ref[...] = jnp.zeros_like(c_ref)
    for head in range(HEADS):
        span, vspan = spans(head)
        query = q_ref[:, span]
        top = None
        for block in range(BLOCKS):
            cols = slice(block * ROWS, block * ROWS + ROWS)
            ref, rows = block_of(refs, block)
            scores = dot_last(query, ref[rows, span]) + bias_ref[:, cols]
            s_ref[:, cols] = scores
            top = scores if top is None else jnp.maximum(top, scores)
        top = jnp.max(top, axis=1, keepdims=True)
        total = jnp.zeros(tile, F32)
        mixed = jnp.zeros((ROWS, HEAD_DIM), F32)
        for block in range(BLOCKS):
            cols = slice(block * ROWS, block * ROWS + ROWS)
            ref, rows = block_of(refs, block)
            weights = jnp.exp(s_ref[:, cols] - top)
            total = total + weights
            mixed = mixed + dot(weights.astype(BF16), ref[rows, vspan])
        total = jnp.sum(total, axis=1, keepdims=True)
        mixed = mixed / total
        o_ref[:, span] = mixed
        ob_ref[:, span] = mixed.astype(BF16)
        c_ref[:, head : head + 1] = top + jnp.log(total)
    l_ref[...] = c_ref[...].T[:8, :]
    copy.wait()
    hidden_pre = dot(a2_ref[...], w[:, :UP]) + v_ref[1:2, :]
    u_ref[...] = hidden_pre
    hidden = gelu(hidden_pre).astype(BF16)
    h_ref[...] = hidden
    out = dot_last(ob_ref[...], w[:, 2 * UP : 2 * UP + ATT]) + dot_last(hidden, w[:, UP : 2 * UP])
    part_ref[...] = out.astype(BF16)


def attend(layer, query, blocks, qs, ks, second_in, vectors, weights):
    return call(
        functools.partial(attend_kernel, layer),
        [
            shape(ROWS, ATT, F32),
            shape(8, ROWS, F32),
            shape(ROWS, UP, F32),
            shape(ROWS, UP, BF16),
            shape(ROWS, ATT, BF16),
            shape(ROWS, WIDTH, BF16),
        ],
        [query, *blocks, qs, ks, second_in, vectors, *weights],
        [VMEM] * 11 + [ANY] * 2,
        [
            pltpu.VMEM((ROWS, BLOCKS * ROWS), F32),
            pltpu.VMEM((ROWS, BLOCKS * ROWS), F32),
            pltpu.VMEM((ROWS, 128), F32),
            pltpu.VMEM((WIDTH, REST), BF16),
            pltpu.SemaphoreType.DMA,
        ],
        2_500_000_000,
        2_000_000,
    )


def residual_kernel(got_ref, x_ref, v_ref, out_ref):
    rank = lax.axis_index("tp")
    total = got_ref[0].astype(F32)
    for index in range(1, 4):
        total = total + got_ref[index].astype(F32)
    rows = x_ref[pl.ds(pl.multiple_of(rank * PART, PART), PART), :].astype(F32)
    result = (rows + total + v_ref[2:3, :]).astype(BF16)
    for index in range(4):
        out_ref[index] = result


def residual(got, x, vectors):
    out = jax.ShapeDtypeStruct((4, PART, WIDTH), BF16)
    return call(residual_kernel, [out], [got, x, vectors], [VMEM] * 3, [], 400_000)[0]


def attend_back_kernel(
    layer, g_ref, o_ref, l_ref, q_ref, b0, b1, b2, b3, b4, br, qs_ref, ks_ref, wa, wb,
    dq_ref, dg_ref, dr_ref, bias_ref, do_ref, c_ref, t_ref, w, sem,
):
    refs = (b0, b1, b2, b3, b4, br)
    copy = pick_start(layer, wa, wb, w, sem, (2 * UP, 256))
    tile = (ROWS, ROWS)
    for block in range(BLOCKS):
        rows = slice(block * ROWS, block * ROWS + ROWS)
        allowed = ks_ref[rows, :] == qs_ref[...]
        if block == BLOCKS - 1:
            keys_of = lax.broadcasted_iota(jnp.int32, tile, 0)
            allowed = allowed & (keys_of <= lax.broadcasted_iota(jnp.int32, tile, 1))
        bias_ref[rows, :] = jnp.where(allowed, 0.0, FAR)
    copy.wait()
    do_ref[...] = dot(g_ref[...], w[:, :ATT]).astype(BF16)
    c_ref[...] = jnp.zeros_like(c_ref)
    for head in range(HEADS):
        span, _ = spans(head)
        product = do_ref[:, span].astype(F32) * o_ref[:, span]
        c_ref[:, head : head + 1] = jnp.sum(product, axis=1, keepdims=True)
    deltas = c_ref[...].T
    t_ref[...] = jnp.zeros_like(t_ref)
    for head in range(HEADS):
        span, vspan = spans(head)
        query = q_ref[:, span]
        grad_out = do_ref[:, span]
        lse = l_ref[head : head + 1, :]
        delta = deltas[head : head + 1, :]
        grad_query = jnp.zeros((HEAD_DIM, ROWS), F32)
        for block in range(BLOCKS):
            ref, rows = block_of(refs, block)
            out = dg_ref if block % 2 == 0 else dr_ref
            place = slice((block // 2) * ROWS, (block // 2) * ROWS + ROWS)
            keys = ref[rows, span]
            scores = dot_last(keys, query) + bias_ref[block * ROWS : block * ROWS + ROWS, :]
            probs = jnp.exp(scores - lse)
            grad_probs = dot_last(ref[rows, vspan], grad_out)
            grad_scores = (probs * (grad_probs - delta)).astype(BF16)
            out[place, span] = dot(grad_scores, query).astype(BF16)
            out[place, vspan] = dot(probs.astype(BF16), grad_out).astype(BF16)
            grad_query = grad_query + dot_first(keys, grad_scores)
        t_ref[span, :] = grad_query * SCALE
    dq_ref[...] = t_ref[...].T[:, :ATT]


def attend_back(layer, grad, mixed, lse, query, blocks, qs, ks, weights):
    return call(
        functools.partial(attend_back_kernel, layer),
        [
            shape(ROWS, ATT, F32),
            shape(5 * ROWS, 2 * ATT, BF16),
            shape(4 * ROWS, 2 * ATT, BF16),
        ],
        [grad, mixed, lse, query, *blocks, qs, ks, *weights],
        [VMEM] * 12 + [ANY] * 2,
        [
            pltpu.VMEM((BLOCKS * ROWS, ROWS), F32),
            pltpu.VMEM((ROWS, ATT), BF16),
            pltpu.VMEM((ROWS, 128), F32),
            pltpu.VMEM((ROWS, ROWS), F32),
            pltpu.VMEM((WIDTH, 256), BF16),
            pltpu.SemaphoreType.DMA,
        ],
        6_000_000_000,
        2_000_000,
    )


def merge_kernel(dg_ref, got_ref, o0, o1, o2, o3, own_ref):
    core = lax.axis_index("section")
    outs = (o0, o1, o2, o3, own_ref)

    def at(ref, block):
        return ref[block * ROWS : block * ROWS + ROWS, :].astype(F32)

    @pl.when(core == 0)
    def _():
        o0[...] = dg_ref[:ROWS, :]
        for block in range(1, 5):
            total = at(dg_ref, block) + at(got_ref, block - 1)
            outs[block][...] = total.astype(outs[block].dtype)

    @pl.when(core == 1)
    def _():
        own_ref[...] = at(dg_ref, 4)
        for block in range(4):
            outs[block][...] = (at(dg_ref, block) + at(got_ref, block)).astype(BF16)


def merge(dg, got):
    outs = [shape(ROWS, 2 * ATT, BF16)] * 4 + [shape(ROWS, 2 * ATT, F32)]
    return call(merge_kernel, outs, [dg, got], [VMEM] * 2, [], 1_000_000)


def hidden_back_kernel(
    layer, g_ref, u_ref, h_ref, a2_ref, n_ref, v_ref, wa, wb, keep_ref, send_ref, e_ref, sums_ref, w, sem
):
    copy = pick_start(layer, wa, wb, w, sem, (0, 2 * UP))
    grad = g_ref[...]
    slope = gelu_slope(u_ref[...])
    copy.wait()
    grad_pre = (dot(grad, w[:, UP:]) * slope).astype(BF16)
    second_grad = dot_last(grad_pre, w[:, :UP])
    e_ref[...] = second_grad * v_ref[4:5, :]
    sums_ref[0:1, :] = jnp.sum(grad_pre.astype(F32), axis=0, keepdims=True)
    sums_ref[1:2, :] = jnp.sum(grad.astype(F32), axis=0, keepdims=True)
    sums_ref[2:3, :] = jnp.sum(second_grad * n_ref[...], axis=0, keepdims=True)
    sums_ref[3:4, :] = jnp.sum(second_grad, axis=0, keepdims=True)
    up = dot_first(a2_ref[...], grad_pre).astype(BF16)
    down = dot_first(grad, h_ref[...]).astype(BF16)
    core = lax.axis_index("section")

    @pl.when(core == 0)
    def _():
        keep_ref[...] = up
        send_ref[...] = down

    @pl.when(core == 1)
    def _():
        keep_ref[...] = down
        send_ref[...] = up


def hidden_back(layer, grad, hidden_pre, hidden, second_in, normed, vectors, weights):
    return call(
        functools.partial(hidden_back_kernel, layer),
        [
            shape(WIDTH, UP, BF16),
            shape(WIDTH, UP, BF16),
            shape(ROWS, WIDTH, F32),
            shape(4, WIDTH, F32),
        ],
        [grad, hidden_pre, hidden, second_in, normed, vectors, *weights],
        [VMEM] * 6 + [ANY] * 2,
        [pltpu.VMEM((WIDTH, 2 * UP), BF16), pltpu.SemaphoreType.DMA],
        1_300_000_000,
        200_000,
    )


def project_back_kernel(
    layer, own_ref, r0, r1, r2, r3, dq_ref, cos_ref, sin_ref, e_ref, n_ref, v_ref, wa, wb,
    dp_ref, part_ref, sums_ref, w, sem,
):
    copy = pick_start(layer, wa, wb, w, sem)
    keyval = own_ref[...]
    for ref in (r0, r1, r2, r3):
        keyval = keyval + ref[...].astype(F32)
    both = jnp.concatenate([dq_ref[...], keyval[:, :ATT]], axis=1)
    both = both * cos_ref[...] - turned(both) * sin_ref[...]
    packed = jnp.concatenate([both, keyval[:, ATT:]], axis=1).astype(BF16)
    dp_ref[...] = packed
    copy.wait()
    first_grad = dot_last(packed, w[...])
    part_ref[...] = (first_grad * v_ref[3:4, :] + e_ref[...]).astype(BF16)
    sums_ref[...] = jnp.zeros_like(sums_ref)
    sums_ref[0:1, :QKV] = jnp.sum(packed.astype(F32), axis=0, keepdims=True)
    sums_ref[1:2, :] = jnp.sum(first_grad * n_ref[...], axis=0, keepdims=True)
    sums_ref[2:3, :] = jnp.sum(first_grad, axis=0, keepdims=True)


def project_back(layer, own, parts, dq, tables, scaled, normed, vectors, weights):
    return call(
        functools.partial(project_back_kernel, layer),
        [shape(ROWS, QKV, BF16), shape(ROWS, WIDTH, BF16), shape(4, WIDTH, F32)],
        [own, *parts, dq, *tables, scaled, normed, vectors, *weights],
        [VMEM] * 11 + [ANY] * 2,
        [pltpu.VMEM((WIDTH, QKV), BF16), pltpu.SemaphoreType.DMA],
        300_000_000,
    )


def late_kernel(a1_ref, dp_ref, g_ref, ob_ref, keep_ref, send_ref):
    first = dot_first(a1_ref[...], dp_ref[...]).astype(BF16)
    out = dot_first(g_ref[...], ob_ref[...]).astype(BF16)
    core = lax.axis_index("section")

    @pl.when(core == 0)
    def _():
        keep_ref[...] = first[:, : 2 * ATT]
        send_ref[:, :ATT] = first[:, 2 * ATT :]
        send_ref[:, ATT:] = out

    @pl.when(core == 1)
    def _():
        send_ref[...] = first[:, : 2 * ATT]
        keep_ref[:, :ATT] = first[:, 2 * ATT :]
        keep_ref[:, ATT:] = out


def late_weights(first_in, packed, grad, mixed):
    return call(
        late_kernel,
        [shape(WIDTH, 2 * ATT, BF16)] * 2,
        [first_in, packed, grad, mixed],
        [VMEM] * 4,
        [],
        300_000_000,
    )


def norm_back_kernel(copies, got_ref, g_ref, n_ref, i_ref, out_ref):
    rank = lax.axis_index("tp")
    rows = pl.ds(pl.multiple_of(rank * PART, PART), PART)
    scaled = got_ref[0].astype(F32)
    for index in range(1, 4):
        scaled = scaled + got_ref[index].astype(F32)
    normed = n_ref[rows, :]
    result = g_ref[rows, :].astype(F32) + i_ref[rows, 0:1] * (
        scaled
        - jnp.mean(scaled, axis=-1, keepdims=True)
        - normed * jnp.mean(scaled * normed, axis=-1, keepdims=True)
    )
    for index in range(copies):
        out_ref[index] = result


def norm_back(copies, got, grad, normed, inverse):
    out = jax.ShapeDtypeStruct((copies, PART, WIDTH), F32)
    ins = [got, grad, normed, inverse]
    return call(functools.partial(norm_back_kernel, copies), [out], ins, [VMEM] * 4, [], 1_000_000)[0]


def rotary_tables(first, count, heads):
    frequency = jnp.exp(-(jnp.arange(ROT // 2, dtype=F32) * (2.0 / ROT)) * jnp.log(10000.0))
    places = (first + jnp.arange(count, dtype=jnp.int32)).astype(F32)
    angles = places[:, None] * frequency[None, :]
    cosine, sine = jnp.cos(angles), jnp.sin(angles)
    ones = jnp.ones((count, HEAD_DIM - ROT), F32)
    zeros = jnp.zeros((count, HEAD_DIM - ROT), F32)
    cos_row = jnp.concatenate([cosine, cosine, ones], 1)
    sin_row = jnp.concatenate([-sine, sine, zeros], 1)
    return jnp.tile(cos_row, (1, heads)), jnp.tile(sin_row, (1, heads))


def tp_exchange(parts):
    return lax.all_to_all(parts, "tp", 0, 0, tiled=True)


def tp_gather(rows):
    return tp_exchange(jnp.broadcast_to(rows[None], (4,) + rows.shape))


def split_up(sums):
    high = sums.astype(BF16)
    return jnp.concatenate([high, (sums - high.astype(F32)).astype(BF16)], 0)


def per_device(
    inputs,
    cotangent,
    segments,
    w_qkv,
    b_qkv,
    w_out,
    w_up,
    b_up,
    w_down,
    b_out,
    norm_gain,
    norm_bias,
):
    core = lax.axis_index("section")
    chip = lax.axis_index("ctx")
    batch = batch_of(chip)
    shard = (chip & ~1) + core
    at_home = (chip % 2) == core
    tokens = inputs.shape[1]
    part_rows = w_qkv.shape[1]

    def by_core(first, second):
        return jnp.where(core == 0, first, second)

    def to_parts(cols):
        lead = cols.shape[:-1]
        return jnp.swapaxes(cols.reshape(lead + (HEADS, 3, HEAD_DIM)), -3, -2).reshape(cols.shape)

    def to_heads(cols):
        lead = cols.shape[:-1]
        return jnp.swapaxes(cols.reshape(lead + (3, HEADS, HEAD_DIM)), -3, -2).reshape(cols.shape)

    seg_row = jnp.concatenate(
        [segments.reshape(1, 2 * tokens).astype(BF16), jnp.zeros((1, QKV - 2 * tokens), BF16)], 1
    )
    piece = jnp.concatenate([to_parts(w_qkv[0]), seg_row, jnp.zeros((7, QKV), BF16)], 0)
    spread = jnp.broadcast_to(piece[None], (CHIPS,) + piece.shape)
    spread = lax.all_to_all(spread, "ctx", 0, 0, tiled=True)
    weight_in = spread[:, :part_rows].reshape(WIDTH, QKV)
    weight_in = (weight_in, swapped(weight_in))
    all_segs = spread[:, part_rows, : 2 * tokens].astype(F32).reshape(CHIPS, 2, tokens)
    all_segs = jnp.where(batch == 0, all_segs[:, 0], all_segs[:, 1]).reshape(CHIPS * tokens)
    all_segs = jnp.concatenate([jnp.full(((BLOCKS - 1) * tokens,), -1.0, F32), all_segs])
    key_segs = lax.dynamic_slice_in_dim(all_segs, shard * tokens, BLOCKS * tokens)
    own_segs = key_segs[(BLOCKS - 1) * tokens :]

    rest = jnp.concatenate(
        [w_up[0], w_down[0], w_out[0], jnp.zeros((part_rows, REST - 2 * UP - ATT), BF16)], 1
    )
    rest = lax.all_gather(rest, "ctx", axis=0, tiled=True)

    away_x = from_home(jnp.where(batch == 0, inputs[1], inputs[0]))
    first_x = jnp.where(at_home, jnp.where(batch == 0, inputs[0], inputs[1]), away_x)
    away_g = from_home(jnp.where(batch == 0, cotangent[1], cotangent[0]))
    last_g = jnp.where(at_home, jnp.where(batch == 0, cotangent[0], cotangent[1]), away_g)

    small = jnp.concatenate(
        [
            jnp.concatenate([to_parts(b_qkv[0]), jnp.zeros((WIDTH - QKV,), BF16)])[None],
            b_up,
            b_out,
            norm_gain[0],
            norm_bias[0],
            jnp.zeros((1, WIDTH), BF16),
        ],
        0,
    )
    other_small = swapped(small)
    vectors = (
        by_core(small, other_small).astype(F32),
        by_core(other_small, small).astype(F32),
    )
    tables = rotary_tables(shard * tokens, tokens, 2 * HEADS)

    def forward(layer, x, rest):
        query, keyval, first_in, second_in, normed, inverse = project(
            layer, x, vectors[layer], tables, weight_in
        )
        blocks = [shifted(keyval, steps) for steps in (4, 3, 2, 1)] + [keyval]
        sent = by_core(jnp.concatenate(blocks[1:], 0), jnp.concatenate(blocks[:-1], 0))
        blocks.append(swapped(sent))
        if layer == 0:
            sent, rest = lax.optimization_barrier((sent, rest))
            rest = (rest, swapped(rest))
        mixed, lse, hidden_pre, hidden, mixed_low, part = attend(
            layer, query, blocks, own_segs[:, None], key_segs[None, :], second_in, vectors[layer], rest
        )
        got = tp_exchange(part.reshape(4, PART, WIDTH))
        result = tp_exchange(residual(got, x, vectors[layer])).reshape(tokens, WIDTH)
        kept = (query, blocks, first_in, second_in, normed, inverse, mixed, lse, hidden_pre, hidden, mixed_low)
        return result, kept, rest

    def spread_sums(keep, send, sums):
        cols = keep.shape[1]
        got = swapped(send)
        total = (keep.astype(F32) + got.astype(F32)).astype(BF16).reshape(CHIPS, part_rows, cols)
        extra = split_up(sums).reshape(1, -1, cols)
        rows = extra.shape[1]
        extra = jnp.broadcast_to(extra, (CHIPS, rows, cols))
        parcel = lax.all_to_all(jnp.concatenate([total, extra], 1), "ctx", 0, 0, tiled=True)
        parcel = jnp.sum(parcel.astype(F32), axis=0)
        sums = parcel[part_rows:].reshape(2, 4, WIDTH)
        return parcel[:part_rows], sums[0] + sums[1]

    def backward(layer, grad, kept):
        query, blocks, first_in, second_in, normed, inverse, mixed, lse, hidden_pre, hidden, mixed_low = kept
        dq, dg, dr = attend_back(
            layer, grad, mixed, lse, query, blocks, own_segs[None, :], key_segs[:, None], rest
        )
        keep, send, scaled, early_sums = hidden_back(
            layer, grad, hidden_pre, hidden, second_in, normed, vectors[layer], rest
        )
        *parts, own = merge(dg, swapped(dr))
        parts = [shifted(part, slot - 4) for slot, part in enumerate(parts)]
        early, early_sums = spread_sums(keep, send, early_sums)
        packed, part, late_sums = project_back(
            layer, own, parts, dq, tables, scaled, normed, vectors[layer], weight_in
        )
        got = tp_exchange(part.reshape(4, PART, WIDTH))
        rows = norm_back(4 if layer else 1, got, grad, normed, inverse)
        keep, send = late_weights(first_in, packed, grad, mixed_low)
        late, late_sums = spread_sums(keep, send, late_sums)
        weight = jnp.concatenate([early, late], 1)
        return rows, weight, jnp.concatenate([early_sums, late_sums], 0)

    first_y, first_kept, rest = forward(0, first_x, rest)
    last_y, last_kept, rest = forward(1, first_y, rest)
    hidden_home = to_home(jnp.stack([first_y, last_y]))

    top_grad, top_weight, top_sums = backward(1, last_g, last_kept)
    top_home = tp_exchange(top_grad).reshape(tokens, WIDTH)
    middle = top_home.astype(BF16)
    top_home = to_home(top_home)

    low_grad, low_weight, low_sums = backward(0, middle, first_kept)
    low_home = tp_gather(to_home(low_grad[0])).reshape(tokens, WIDTH)

    def norm_rows(sums):
        return jnp.concatenate([sums[5:6], sums[2:3], sums[6:7], sums[3:4]], 0)

    norms = jnp.concatenate([norm_rows(low_sums), norm_rows(top_sums)], 0)
    norms = jnp.sum(tp_gather(norms), axis=0)

    def two_batches(layers):
        mine = by_core(layers[0], layers[1])
        got = swapped(by_core(layers[1], layers[0]))
        return jnp.stack([by_core(mine, got), by_core(got, mine)])

    hidden_out = two_batches(hidden_home)[None]
    input_grad = two_batches((low_home, top_home))[None]
    low_all = jnp.concatenate([low_sums, norms[:4]], 0)
    top_all = jnp.concatenate([top_sums, norms[4:]], 0)
    sums = by_core(low_all, top_all) + swapped(by_core(top_all, low_all))
    mine = by_core(low_weight, top_weight)
    got = swapped(by_core(top_weight, low_weight))
    left, right = by_core(mine, got), by_core(got, mine)
    grad_in = jnp.concatenate([left[:, UP:], right[:, UP : UP + ATT]], 1)
    return (
        hidden_out,
        input_grad,
        to_heads(grad_in)[None],
        to_heads(sums[4, :QKV])[None],
        right[:, UP + ATT :][None],
        left[:, :UP][None],
        sums[0][None],
        right[:, :UP][None],
        sums[1][None],
        sums[8:10][None],
        sums[10:12][None],
    )


def solution(mesh):
    placed = (
        P(None, "ctx", None),
        P(None, "ctx", None),
        P(None, "ctx"),
        P("section", "ctx", "tp"),
        P("section", "tp"),
        P("section", "ctx", "tp"),
        P("section", "ctx", "tp"),
        P("section", "tp"),
        P("section", "ctx", "tp"),
        P("section", None),
        P("section", None, None),
        P("section", None, None),
    )
    return jax.shard_map(
        per_device,
        mesh=mesh,
        in_specs=placed,
        out_specs=(
            P("section", None, "ctx", None),
            P("section", None, "ctx", None),
            P("section", "ctx", "tp"),
            P("section", "tp"),
            P("section", "ctx", "tp"),
            P("section", "ctx", "tp"),
            P("section", "tp"),
            P("section", "ctx", "tp"),
            P("section", None),
            P("section", None, None),
            P("section", None, None),
        ),
        check_vma=False,
    )
```
